256 devices in a mesh: replica: 32 (over y, z), tensor: 8 (over x, core).
Axes of the slice: x: 4, y: 4, z: 8, core: 2. Of those that a mesh axis runs over, the one named last changes fastest.
Arguments:
- inputs: bfloat16 [8192, 2560], P(('replica', 'tensor')), may hold values from -6 to 6
- pre_act: bfloat16 [8192, 7936], P('replica', 'tensor'), may hold values from -8 to 8
- grad_hidden: bfloat16 [8192, 7936], P('replica', 'tensor'), may hold values from -1.75 to 1.75
- up_weight: bfloat16 [2560, 7936], P('replica', 'tensor'), may hold values from -0.125 to 0.125
- error_in: bfloat16 [32, 2560, 7936], P('replica', None, 'tensor'), may hold values from -12 to 12
- q_prev: float32 [7936, 128], P('tensor'), may hold values from -0.0625 to 0.0625
Outputs:
- input_grad: bfloat16 [8192, 2560], P(('replica', 'tensor'))
- q_factor: float32 [7936, 128], P('tensor')
- error_out: bfloat16 [32, 2560, 7936], P('replica', None, 'tensor')
The draws below stay inside these ranges and needn't reach their ends.
All inputs are finite; a program needn't handle non-finite values.
Results may differ from the reference program's by a relative error of at most 0.02.
Values may be sent and summed in bfloat16 or wider, within the bound.
No kernel may reach another device: no remote copies, remote signals or barrier semaphores. Data moves between devices by JAX's collectives and lax.ppermute only.
A program may use at most 128 MiB of HBM per device.

```python
import jax
import jax.numpy as jnp
from jax import lax

DW = 2560
FF = 7936
RANK = 128
TOK = 256
REPLICAS = 32
ROWS = 8192


def block_levels(stream_key, shape, split, least, top_value):
    level = 1.0
    for position, parts in split:
        steps = jax.random.uniform(jax.random.fold_in(jax.random.fold_in(stream_key, 6), position), (parts,), jnp.float32, least / len(split), top_value / len(split))
        level = level * jnp.repeat(jnp.exp(steps), shape[position] // parts).reshape((-1,) + (1,) * (len(shape) - 1 - position))
    return level


def gaussian(stream_key, dims, scale, bound, pieces=(), kind=jnp.bfloat16):
    gain = block_levels(stream_key, dims, pieces, -0.22, 0.18) if pieces else 1.0
    values = jax.random.normal(stream_key, dims, jnp.float32) * scale * gain
    return jnp.minimum(jnp.maximum(values, -bound), bound).astype(kind)


def setup_inputs(seed: int = 0) -> dict:
    key_of = jax.random.split(jax.random.key(seed), 7)
    inputs = gaussian(key_of[0], (ROWS, DW), 1.0, 6.0, ((0, 256),))
    pre_act = gaussian(key_of[1], (ROWS, FF), 1.5, 8.0, ((0, 32), (1, 8)))
    grad_hidden = gaussian(key_of[2], (ROWS, FF), 0.3, 1.75, ((0, 32), (1, 8)))
    up_weight = gaussian(key_of[3], (DW, FF), DW ** -0.5, 0.125, ((0, 32), (1, 8)))
    error_in = gaussian(key_of[4], (REPLICAS, DW, FF), 2.0, 12.0, ((0, 32), (2, 8)))
    q_prev = gaussian(key_of[5], (FF, RANK), FF ** -0.5, 0.0625, ((0, 8),), jnp.float32)
    return {"inputs": inputs, "pre_act": pre_act, "grad_hidden": grad_hidden, "up_weight": up_weight, "error_in": error_in, "q_prev": q_prev}


precise = lax.Precision.HIGHEST
root_half = 0.7071067811865476
inverse_root = 0.3989422804014327

def hidden_slope(pre_act, grad_hidden):
    values = pre_act.astype(jnp.float32)
    normal_cdf = 0.5 * (1.0 + jax.scipy.special.erf(values * root_half))
    density = jnp.exp(-0.5 * values * values) * inverse_root
    return (grad_hidden.astype(jnp.float32) * (normal_cdf + values * density)).astype(jnp.bfloat16)

def orthonormal(basis_sum):
    gram_matrix = jnp.dot(basis_sum.T.astype(jnp.float32), basis_sum.astype(jnp.float32), precision=precise, preferred_element_type=jnp.float32)
    factor = jnp.linalg.cholesky(gram_matrix)
    return jax.scipy.linalg.solve_triangular(factor, basis_sum.T, lower=True).T

def reference(inputs, pre_act, grad_hidden, up_weight, error_in, q_prev):
    slopes = hidden_slope(pre_act, grad_hidden)
    input_grad = jnp.dot(slopes.astype(jnp.float32), up_weight.T.astype(jnp.float32), preferred_element_type=jnp.float32).astype(jnp.bfloat16)
    token_rows = inputs.reshape(REPLICAS, TOK, DW)
    slope_rows = slopes.reshape(REPLICAS, TOK, FF)
    operands = (token_rows, slope_rows, error_in)

    def combine(token_block, slope_block, error_block):
        product = jnp.dot(token_block.T.astype(jnp.float32), slope_block.astype(jnp.float32), preferred_element_type=jnp.float32)
        return product + error_block.astype(jnp.float32)

    def basis_term(operand):
        return jnp.dot(combine(*operand).astype(jnp.float32), q_prev.astype(jnp.float32), precision=precise, preferred_element_type=jnp.float32)
    basis_sum = jnp.sum(lax.map(basis_term, operands), axis=0) / REPLICAS
    orthogonal = orthonormal(basis_sum)

    def factor_term(operand):
        return jnp.dot(combine(*operand).T.astype(jnp.float32), orthogonal.astype(jnp.float32), precision=precise, preferred_element_type=jnp.float32)
    q_factor = jnp.sum(lax.map(factor_term, operands), axis=0) / REPLICAS
    approx = jnp.dot(orthogonal.astype(jnp.float32), q_factor.T.astype(jnp.float32), precision=precise, preferred_element_type=jnp.float32)

    def residual_term(operand):
        return (combine(*operand) - approx).astype(jnp.bfloat16)
    error_out = lax.map(residual_term, operands)
    return (input_grad, q_factor, error_out)
```

```python
import jax
import jax.numpy as jnp
from jax import lax
from jax.sharding import PartitionSpec as P

f32, bf16 = jnp.float32, jnp.bfloat16
precise = lax.Precision.HIGHEST
root_half = 0.7071067811865476
inverse_root = 0.3989422804014327

RANK = 128
CORE_PAIRS = [(i, i ^ 1) for i in range(8)]
CHIP_GROUPS = [[core + 2 * chip for chip in range(4)] for core in range(2)]


def hidden_slope(pre_act, grad_hidden):
    values = pre_act.astype(f32)
    normal_cdf = 0.5 * (1.0 + jax.scipy.special.erf(values * root_half))
    density = jnp.exp(-0.5 * values * values) * inverse_root
    return (grad_hidden.astype(f32) * (normal_cdf + values * density)).astype(bf16)


def split(values):
    high = lax.reduce_precision(values, 8, 7)
    return high.astype(bf16), (values - high).astype(bf16)


def dot(left, right, left_dim, right_dim):
    return lax.dot_general(
        left, right, (((left_dim,), (right_dim,)), ((), ())), preferred_element_type=f32
    )


def dot_pair(left, right, left_dim):
    both = dot(left, jnp.concatenate(split(right), axis=1), left_dim, 0)
    return both[:, :RANK] + both[:, RANK:]


def reduce_tensor(values):
    core = lax.axis_index("tensor") % 2
    half = values.shape[0] // 2
    halves = values.reshape(2, half, RANK)
    kept = lax.dynamic_index_in_dim(halves, core, 0, keepdims=False)
    sent = lax.dynamic_index_in_dim(halves, 1 - core, 0, keepdims=False)
    kept = kept + lax.ppermute(sent, "tensor", CORE_PAIRS)
    blocks = lax.all_to_all(
        kept.reshape(4, half // 4, RANK), "tensor", 0, 0, axis_index_groups=CHIP_GROUPS
    )
    return jnp.sum(blocks, axis=0)


def gather_tensor(rows):
    blocks = lax.all_to_all(
        jnp.broadcast_to(rows[None], (4, *rows.shape)),
        "tensor",
        0,
        0,
        axis_index_groups=CHIP_GROUPS,
    )
    mine = blocks.reshape(-1, RANK)
    other = lax.ppermute(mine, "tensor", CORE_PAIRS)
    first = lax.axis_index("tensor") % 2 == 0
    return jnp.concatenate([jnp.where(first, mine, other), jnp.where(first, other, mine)], axis=0)


def reduce_replica(values, rows):
    padded = jnp.pad(values, ((0, 32 * rows - values.shape[0]), (0, 0))).reshape(32, rows, RANK)
    return jnp.sum(lax.all_to_all(padded, "replica", 0, 0).astype(f32), axis=0)


def gather_replica(block, count):
    blocks = lax.all_to_all(jnp.broadcast_to(block[None], (32, *block.shape)), "replica", 0, 0)
    return blocks.reshape(-1, RANK)[:count]


def on_device(inputs, pre_act, grad_hidden, up_weight, error_in, q_prev):
    replicas = lax.axis_size("replica")
    error = error_in[0]
    weights = lax.all_gather(up_weight, "replica", axis=0, tiled=True)
    tokens = lax.all_gather(inputs, "tensor", axis=0, tiled=True)
    slopes = hidden_slope(pre_act, grad_hidden)
    with jax.named_scope("basis"):
        slope_terms = dot_pair(slopes, q_prev, 1)
        own_slopes = jnp.sum(
            lax.all_to_all(slope_terms.reshape(8, -1, RANK), "tensor", 0, 0), axis=0
        )
        basis_terms = dot_pair(error, q_prev, 1) + dot_pair(inputs, own_slopes, 0)
        rows = reduce_tensor(basis_terms)
        rows = reduce_replica(rows, 16) / replicas
        basis_sum = gather_tensor(gather_replica(rows, 320))
    with jax.named_scope("orthonormal"):
        gram_matrix = jnp.dot(basis_sum.T, basis_sum, precision=precise, preferred_element_type=f32)
        factor = jnp.linalg.cholesky(gram_matrix)
        orthogonal = jax.scipy.linalg.solve_triangular(factor, basis_sum.T, lower=True).T
    with jax.named_scope("right_factor"):
        local_factor = dot_pair(error, orthogonal, 0) + dot_pair(
            slopes, dot_pair(tokens, orthogonal, 1), 0
        )
        block = reduce_replica(local_factor.astype(bf16), 32) / replicas
        q_factor = gather_replica(block.astype(bf16), 992).astype(f32)
    with jax.named_scope("residual"):
        p_high, p_low = split(orthogonal)
        q_high = q_factor.astype(bf16)
        approx = dot(
            jnp.concatenate([p_high, p_low], axis=1),
            jnp.concatenate([q_high, q_high], axis=1),
            1,
            1,
        )
        error_out = (dot(tokens, slopes, 0, 0) + error.astype(f32) - approx).astype(bf16)[None]
    with jax.named_scope("input_grad"):
        partial_grad = dot(slopes, weights, 1, 1)
        input_grad = lax.psum_scatter(
            partial_grad, "tensor", scatter_dimension=0, tiled=True
        ).astype(bf16)
    return (input_grad, q_factor, error_out)


def solution(mesh):
    placed = (
        P(("replica", "tensor"), None),
        P("replica", "tensor"),
        P("replica", "tensor"),
        P("replica", "tensor"),
        P("replica", None, "tensor"),
        P("tensor", None),
    )
    return jax.shard_map(
        on_device,
        mesh=mesh,
        in_specs=placed,
        out_specs=(P(("replica", "tensor"), None), P("tensor", None), P("replica", None, "tensor")),
        check_vma=False,
    )
```

```python
import jax
import jax.numpy as jnp
from jax import lax
from jax.experimental import pallas as pl
from jax.experimental.pallas import tpu as pltpu
from jax.sharding import PartitionSpec as P

f32, bf16 = jnp.float32, jnp.bfloat16
precise = lax.Precision.HIGHEST
root_half = 0.7071067811865476
inverse_root = 0.3989422804014327

RANK = 128
DW = 2560
HALF = DW // 2
HIDDEN = 992
TILE = 256
CORE_PAIRS = [(i, i ^ 1) for i in range(8)]
X_GROUPS = [[core + 2 * x for x in range(4)] for core in range(2)]
XY_GROUPS = [
    [((y * 8 + z) * 4 + x) * 2 + core for y in range(4) for x in range(4)]
    for z in range(8)
    for core in range(2)
]
Z_GROUPS = [[y * 8 + z for z in range(8)] for y in range(4)]
BOTH = ("replica", "tensor")


def hidden_slope(pre_act, grad_hidden):
    values = pre_act.astype(f32)
    normal_cdf = 0.5 * (1.0 + jax.scipy.special.erf(values * root_half))
    density = jnp.exp(-0.5 * values * values) * inverse_root
    return (grad_hidden.astype(f32) * (normal_cdf + values * density)).astype(bf16)


def dot(left, right, left_dim, right_dim, precision=None):
    return lax.dot_general(
        left,
        right,
        (((left_dim,), (right_dim,)), ((), ())),
        precision=precision,
        preferred_element_type=f32,
    )


def split_outside(values):
    high = lax.reduce_precision(values, 8, 7)
    return jnp.concatenate([high.astype(bf16), (values - high).astype(bf16)], axis=1)


def split(values):
    high = values.astype(bf16)
    return jnp.concatenate([high, (values - high.astype(f32)).astype(bf16)], axis=1)


def folded(both):
    return both[:, :RANK] + both[:, RANK:]


def broadcast_exchange(block, count, axis, groups=None):
    blocks = jnp.broadcast_to(block[None], (count, *block.shape))
    return lax.all_to_all(blocks, axis, 0, 0, axis_index_groups=groups)


def whole(shape, memory=pltpu.VMEM):
    return pl.BlockSpec(shape, lambda *_: (0,) * len(shape), memory_space=memory)


def terms_kernel(core_ref, mine_ref, other_ref, z_ref, error_ref, kept_ref, sent_ref, tokens_ref):
    core = core_ref[0]
    for x in range(4):
        for ref, owner in ((mine_ref, core), (other_ref, 1 - core)):
            start = pl.multiple_of((2 * x + owner) * 32, 32)
            tokens_ref[pl.ds(start, 32), :] = ref[x]
    both = split(z_ref[...])
    for ref, part in ((kept_ref, core), (sent_ref, 1 - core)):
        start = pl.multiple_of(part * HALF, HALF)
        columns = tokens_ref[:, pl.ds(start, HALF)]
        ref[...] = folded(dot(columns, both, 0, 0)) + error_ref[pl.ds(start, HALF), :]


def left_terms(core, mine, other, slope_terms, error_terms):
    return pl.pallas_call(
        terms_kernel,
        out_shape=(
            jax.ShapeDtypeStruct((HALF, RANK), f32),
            jax.ShapeDtypeStruct((HALF, RANK), f32),
            jax.ShapeDtypeStruct((256, DW), bf16),
        ),
        in_specs=[pl.BlockSpec(memory_space=pltpu.SMEM)]
        + [pl.BlockSpec(memory_space=pltpu.VMEM)] * 4,
        out_specs=[pl.BlockSpec(memory_space=pltpu.VMEM)] * 3,
        compiler_params=pltpu.CompilerParams(vmem_limit_bytes=32 * 2**20),
        cost_estimate=pl.CostEstimate(
            flops=2 * 256 * DW * 256, bytes_accessed=6_000_000, transcendentals=0
        ),
        name="left_terms",
    )(core, mine, other, slope_terms, error_terms)


def invert_factor(gram, work_ref, out_ref):
    sub = lax.broadcasted_iota(jnp.int32, (8, RANK), 0)
    lane = lax.broadcasted_iota(jnp.int32, (8, RANK), 1)
    work_ref[...] = gram

    def spread(rows, column):
        return jnp.broadcast_to(rows[:, column : column + 1], (8, RANK))

    def row(values, k):
        return jnp.broadcast_to(values[k : k + 1, :], (8, RANK))

    current = work_ref[0:8, :]
    for r in range(16):
        base = 8 * r
        last = r == 15
        inside = (lane >= base) & (lane < base + 8)
        columns = [spread(current, base + k) for k in range(8)]
        current = jnp.where(inside, jnp.where(lane - base == sub, 1.0, 0.0), current)
        if not last:
            after = work_ref[base + 8 : base + 16, :]
            after_columns = [spread(after, base + k) for k in range(8)]
            after = jnp.where(inside, 0.0, after)
        inverse = jnp.zeros((8, RANK), f32)
        for k in range(8):
            pivot_inverse = 1.0 / row(columns[k], k)
            ratio = jnp.where(sub > k, columns[k] * pivot_inverse, 0.0)
            inverse = jnp.where(sub == k, pivot_inverse, inverse)
            pivot_row = row(current, k)
            current = current - ratio * pivot_row
            tops = {i: row(columns[i], k) for i in range(k + 1, 8)}
            for i in range(k + 1, 8):
                columns[i] = columns[i] - ratio * tops[i]
            if not last:
                ratio = after_columns[k] * pivot_inverse
                for i in range(k + 1, 8):
                    after_columns[i] = after_columns[i] - ratio * tops[i]
                after = after - ratio * pivot_row
        out_ref[base : base + 8, :] = jnp.where(lane < base + 8, current * lax.sqrt(inverse), 0.0)
        if r < 14:
            top = base + 16
            scaled = jnp.where(lane >= top, current * inverse, 0.0)
            update = dot(scaled, current, 0, 0, precise)
            lanes = lax.broadcasted_iota(jnp.int32, (RANK - top, RANK), 1)
            rest = jnp.where((lanes >= base) & (lanes < base + 8), 0.0, work_ref[top:, :])
            work_ref[top:, :] = rest - update[top:, :]
        if not last:
            current = after


def orthonormal_kernel(core_ref, mine_ref, other_ref, out_ref, work_ref, inverse_ref):
    core = core_ref[0]
    mine, other = mine_ref[...], other_ref[...]
    gram = dot(mine, mine, 0, 0, precise) + dot(other, other, 0, 0, precise)
    invert_factor(gram, work_ref, inverse_ref)
    inverse = inverse_ref[...]
    for ref, part in ((mine_ref, core), (other_ref, 1 - core)):
        start = pl.multiple_of(part * HALF, HALF)
        out_ref[pl.ds(start, HALF), :] = split(dot(ref[...], inverse, 1, 1, precise))


def orthonormal(core, mine, other):
    return pl.pallas_call(
        orthonormal_kernel,
        out_shape=jax.ShapeDtypeStruct((DW, 2 * RANK), bf16),
        in_specs=[pl.BlockSpec(memory_space=pltpu.SMEM)]
        + [pl.BlockSpec(memory_space=pltpu.VMEM)] * 2,
        out_specs=pl.BlockSpec(memory_space=pltpu.VMEM),
        scratch_shapes=[pltpu.VMEM((RANK, RANK), f32), pltpu.VMEM((RANK, RANK), f32)],
        compiler_params=pltpu.CompilerParams(vmem_limit_bytes=32 * 2**20),
        cost_estimate=pl.CostEstimate(
            flops=2_000_000_000, bytes_accessed=4_000_000, transcendentals=256
        ),
        name="orthonormal",
    )(core, mine, other)


def factor_kernel(error_ref, slopes_ref, tokens_ref, p_ref, out_ref, y_ref):
    step = pl.program_id(0)

    @pl.when(step == 0)
    def _():
        y_ref[...] = split(folded(dot(tokens_ref[...], p_ref[...], 1, 0)))

    terms = dot(error_ref[...], p_ref[...], 1, 0) + dot(slopes_ref[...], y_ref[...], 1, 0)
    rows = lax.broadcasted_iota(jnp.int32, (TILE, RANK), 0) + step * TILE
    out_ref[...] = jnp.where(rows < HIDDEN, folded(terms), 0.0).astype(bf16)


def factor_terms(error, slopes, tokens, p_both):
    return pl.pallas_call(
        factor_kernel,
        grid=(4,),
        out_shape=jax.ShapeDtypeStruct((4 * TILE, RANK), bf16),
        in_specs=[
            pl.BlockSpec((TILE, DW), lambda i: (i, 0)),
            pl.BlockSpec((TILE, 256), lambda i: (i, 0)),
            whole((256, DW)),
            whole((DW, 2 * RANK)),
        ],
        out_specs=pl.BlockSpec((TILE, RANK), lambda i: (i, 0)),
        scratch_shapes=[pltpu.VMEM((256, 2 * RANK), bf16)],
        compiler_params=pltpu.CompilerParams(vmem_limit_bytes=32 * 2**20),
        cost_estimate=pl.CostEstimate(
            flops=2 * 1024 * DW * 256, bytes_accessed=8_000_000, transcendentals=0
        ),
        name="factor_terms",
    )(error, slopes, tokens, p_both)


def residual_kernel(error_ref, slopes_ref, tokens_ref, p_ref, q_ref, out_ref, factor_ref):
    q = q_ref[...]
    factor_ref[...] = q.astype(f32)
    values = error_ref[...].astype(f32) + dot(slopes_ref[...], tokens_ref[...], 1, 0)
    values = values - dot(jnp.concatenate([q, q], axis=1), p_ref[...], 1, 1)
    out_ref[...] = values.astype(bf16)


def residual(error, slopes, tokens, p_both, q_factor):
    return pl.pallas_call(
        residual_kernel,
        grid=(4,),
        out_shape=(
            jax.ShapeDtypeStruct((HIDDEN, DW), bf16),
            jax.ShapeDtypeStruct((HIDDEN, RANK), f32),
        ),
        in_specs=[
            pl.BlockSpec((TILE, DW), lambda i: (i, 0)),
            pl.BlockSpec((TILE, 256), lambda i: (i, 0)),
            whole((256, DW)),
            whole((DW, 2 * RANK)),
            pl.BlockSpec((TILE, RANK), lambda i: (i, 0)),
        ],
        out_specs=[
            pl.BlockSpec((TILE, DW), lambda i: (i, 0)),
            pl.BlockSpec((TILE, RANK), lambda i: (i, 0)),
        ],
        compiler_params=pltpu.CompilerParams(vmem_limit_bytes=48 * 2**20),
        cost_estimate=pl.CostEstimate(
            flops=4 * 1024 * DW * 256, bytes_accessed=14_000_000, transcendentals=0
        ),
        name="residual",
    )(error, slopes, tokens, p_both, q_factor)


def on_device(inputs, pre_act, grad_hidden, up_weight, error_in, q_prev):
    replicas = lax.axis_size("replica")
    core = (lax.axis_index("tensor") % 2).astype(jnp.int32)
    flag = core.reshape(1)
    error = error_in[0].T
    with jax.named_scope("gathers"):
        weights = lax.all_gather(up_weight, "replica", axis=0, tiled=True)
        mine = broadcast_exchange(inputs, 4, "tensor", X_GROUPS)
        other = lax.ppermute(mine, "tensor", CORE_PAIRS)
    with jax.named_scope("basis"):
        slopes = hidden_slope(pre_act.T, grad_hidden.T)
        q_both = split_outside(q_prev)
        slope_terms = folded(dot(slopes, q_both, 0, 0))
        error_terms = folded(dot(error, q_both, 0, 0))
        kept, sent, tokens = left_terms(flag, mine, other, slope_terms, error_terms)
        kept = kept + lax.ppermute(sent, "tensor", CORE_PAIRS)
        rows = lax.all_to_all(
            kept.reshape(16, HALF // 16, RANK), BOTH, 0, 0, axis_index_groups=XY_GROUPS
        )
        rows = jnp.sum(rows, axis=0)
        rows = jnp.sum(broadcast_exchange(rows, 8, "replica", Z_GROUPS), axis=0) / replicas
        mine = broadcast_exchange(rows, 16, BOTH, XY_GROUPS).reshape(HALF, RANK)
        other = lax.ppermute(mine, "tensor", CORE_PAIRS)
    p_both = orthonormal(flag, mine, other)
    with jax.named_scope("right_factor"):
        terms = factor_terms(error, slopes, tokens, p_both).reshape(32, 32, RANK)
        terms = lax.all_to_all(terms, "replica", 0, 0)
        block = jnp.sum(terms.astype(f32), axis=0) / replicas
        q_block = broadcast_exchange(block.astype(bf16), 32, "replica").reshape(1024, RANK)
    error_out, q_factor = residual(error, slopes, tokens, p_both, q_block)
    with jax.named_scope("input_grad"):
        partial_grad = dot(slopes, weights, 0, 1).reshape(4, 2, 32, DW)
        own = lax.dynamic_index_in_dim(partial_grad, core, 1, keepdims=False)
        pair = lax.dynamic_index_in_dim(partial_grad, 1 - core, 1, keepdims=False)
        own = (own + lax.ppermute(pair, "tensor", CORE_PAIRS)).reshape(128, DW)
        input_grad = lax.psum_scatter(
            own, "tensor", scatter_dimension=0, tiled=True, axis_index_groups=X_GROUPS
        ).astype(bf16)
    return (input_grad, q_factor, error_out.T[None])


def solution(mesh):
    placed = (
        P(("replica", "tensor"), None),
        P("replica", "tensor"),
        P("replica", "tensor"),
        P("replica", "tensor"),
        P("replica", None, "tensor"),
        P("tensor", None),
    )
    return jax.shard_map(
        on_device,
        mesh=mesh,
        in_specs=placed,
        out_specs=(P(("replica", "tensor"), None), P("tensor", None), P("replica", None, "tensor")),
        check_vma=False,
    )
```

```python
import jax
import jax.numpy as jnp
from jax import lax
from jax.experimental import pallas as pl
from jax.experimental.pallas import tpu as pltpu
from jax.sharding import PartitionSpec as P

f32, bf16 = jnp.float32, jnp.bfloat16
precise = lax.Precision.HIGHEST
root_half = 0.7071067811865476
inverse_root = 0.3989422804014327

RANK = 128
DW = 2560
HALF = DW // 2
HIDDEN = 992
TILE = 256
LARGE = 60 * 2**20
CORE_PAIRS = [(i, i ^ 1) for i in range(8)]
X_GROUPS = [[core + 2 * x for x in range(4)] for core in range(2)]
XY_GROUPS = [
    [((y * 8 + z) * 4 + x) * 2 + core for y in range(4) for x in range(4)]
    for z in range(8)
    for core in range(2)
]
Z_GROUPS = [[y * 8 + z for z in range(8)] for y in range(4)]
BOTH = ("replica", "tensor")


def hidden_slope(pre_act, grad_hidden):
    values = pre_act.astype(f32)
    normal_cdf = 0.5 * (1.0 + jax.scipy.special.erf(values * root_half))
    density = jnp.exp(-0.5 * values * values) * inverse_root
    return (grad_hidden.astype(f32) * (normal_cdf + values * density)).astype(bf16)


def dot(left, right, left_dim, right_dim, precision=None):
    return lax.dot_general(
        left,
        right,
        (((left_dim,), (right_dim,)), ((), ())),
        precision=precision,
        preferred_element_type=f32,
    )


def split_outside(values):
    high = lax.reduce_precision(values, 8, 7)
    return jnp.concatenate([high.astype(bf16), (values - high).astype(bf16)], axis=1)


def split(values):
    high = values.astype(bf16)
    return jnp.concatenate([high, (values - high.astype(f32)).astype(bf16)], axis=1)


def folded(both):
    return both[:, :RANK] + both[:, RANK:]


def broadcast_exchange(block, count, axis, groups=None):
    blocks = jnp.broadcast_to(block[None], (count, *block.shape))
    return lax.all_to_all(blocks, axis, 0, 0, axis_index_groups=groups)


def whole(shape, memory=pltpu.VMEM):
    return pl.BlockSpec(shape, lambda *_: (0,) * len(shape), memory_space=memory)


def after(values, order):
    return pl.pallas_call(
        lambda values_ref, order_ref, out_ref: None,
        out_shape=jax.ShapeDtypeStruct(values.shape, values.dtype),
        in_specs=[pl.BlockSpec(memory_space=pl.ANY)] * 2,
        out_specs=pl.BlockSpec(memory_space=pl.ANY),
        input_output_aliases={0: 0},
        cost_estimate=pl.CostEstimate(flops=1000, bytes_accessed=1000, transcendentals=0),
        name="after",
    )(values, order)


def front_kernel(core_ref, error_ref, slopes_ref, q_ref, error_out_ref, own_ref, pair_ref, z_ref):
    core = core_ref[0]

    @pl.when(pl.program_id(0) == 0)
    def _():
        z_ref[...] = folded(dot(slopes_ref[...], q_ref[...], 0, 0))
        for x in range(4):
            for ref, owner in ((own_ref, core), (pair_ref, 1 - core)):
                start = pl.multiple_of((2 * x + owner) * 32, 32)
                ref[32 * x : 32 * x + 32, :] = z_ref[pl.ds(start, 32), :]

    error_out_ref[...] = folded(dot(error_ref[...], q_ref[...], 0, 0))


def front_terms(core, error, slopes, q_both):
    here = pl.BlockSpec(memory_space=pltpu.VMEM)
    return pl.pallas_call(
        front_kernel,
        grid=(5,),
        out_shape=(
            jax.ShapeDtypeStruct((DW, RANK), f32),
            jax.ShapeDtypeStruct((128, RANK), f32),
            jax.ShapeDtypeStruct((128, RANK), f32),
        ),
        in_specs=[
            pl.BlockSpec(memory_space=pltpu.SMEM),
            pl.BlockSpec((HIDDEN, 512), lambda i: (0, i)),
            here,
            here,
        ],
        out_specs=[pl.BlockSpec((512, RANK), lambda i: (i, 0)), here, here],
        scratch_shapes=[pltpu.VMEM((256, RANK), f32)],
        compiler_params=pltpu.CompilerParams(vmem_limit_bytes=LARGE),
        cost_estimate=pl.CostEstimate(
            flops=2 * HIDDEN * DW * 256, bytes_accessed=7_000_000, transcendentals=0
        ),
        name="front_terms",
    )(core, error, slopes, q_both)


def terms_kernel(core_ref, mine_ref, own_ref, got_ref, error_ref, kept_ref, sent_ref):
    core = core_ref[0]
    both = split(own_ref[...] + got_ref[...])
    for ref, part in ((kept_ref, core), (sent_ref, 1 - core)):
        start = pl.multiple_of(part * HALF, HALF)
        columns = mine_ref[:, pl.ds(start, HALF)]
        ref[...] = folded(dot(columns, both, 0, 0)) + error_ref[pl.ds(start, HALF), :]


def left_terms(core, mine, own, got, errors):
    return pl.pallas_call(
        terms_kernel,
        out_shape=(
            jax.ShapeDtypeStruct((HALF, RANK), f32),
            jax.ShapeDtypeStruct((HALF, RANK), f32),
        ),
        in_specs=[pl.BlockSpec(memory_space=pltpu.SMEM)]
        + [pl.BlockSpec(memory_space=pltpu.VMEM)] * 4,
        out_specs=[pl.BlockSpec(memory_space=pltpu.VMEM)] * 2,
        compiler_params=pltpu.CompilerParams(vmem_limit_bytes=20 * 2**20),
        cost_estimate=pl.CostEstimate(
            flops=2 * 128 * DW * 256, bytes_accessed=4_000_000, transcendentals=0
        ),
        name="left_terms",
    )(core, mine, own, got, errors)


def invert_factor(gram, work_ref, out_ref):
    sub = lax.broadcasted_iota(jnp.int32, (8, RANK), 0)
    lane = lax.broadcasted_iota(jnp.int32, (8, RANK), 1)
    work_ref[...] = gram

    def spread(rows, column):
        return jnp.broadcast_to(rows[:, column : column + 1], (8, RANK))

    def row(values, k):
        return jnp.broadcast_to(values[k : k + 1, :], (8, RANK))

    current = work_ref[0:8, :]
    for r in range(16):
        base = 8 * r
        last = r == 15
        inside = (lane >= base) & (lane < base + 8)
        columns = [spread(current, base + k) for k in range(8)]
        current = jnp.where(inside, jnp.where(lane - base == sub, 1.0, 0.0), current)
        if not last:
            after = work_ref[base + 8 : base + 16, :]
            after_columns = [spread(after, base + k) for k in range(8)]
            after = jnp.where(inside, 0.0, after)
        inverse = jnp.zeros((8, RANK), f32)
        for k in range(8):
            pivot_inverse = 1.0 / row(columns[k], k)
            ratio = jnp.where(sub > k, columns[k] * pivot_inverse, 0.0)
            inverse = jnp.where(sub == k, pivot_inverse, inverse)
            pivot_row = row(current, k)
            current = current - ratio * pivot_row
            tops = {i: row(columns[i], k) for i in range(k + 1, 8)}
            for i in range(k + 1, 8):
                columns[i] = columns[i] - ratio * tops[i]
            if not last:
                ratio = after_columns[k] * pivot_inverse
                for i in range(k + 1, 8):
                    after_columns[i] = after_columns[i] - ratio * tops[i]
                after = after - ratio * pivot_row
        out_ref[base : base + 8, :] = jnp.where(lane < base + 8, current * lax.sqrt(inverse), 0.0)
        if r < 14:
            top = base + 16
            scaled = jnp.where(lane >= top, current * inverse, 0.0)
            update = dot(scaled, current, 0, 0, precise)
            lanes = lax.broadcasted_iota(jnp.int32, (RANK - top, RANK), 1)
            rest = jnp.where((lanes >= base) & (lanes < base + 8), 0.0, work_ref[top:, :])
            work_ref[top:, :] = rest - update[top:, :]
        if not last:
            current = after


def orthonormal_kernel(core_ref, mine_ref, other_ref, out_ref, work_ref, inverse_ref):
    core = core_ref[0]
    mine, other = mine_ref[...], other_ref[...]
    gram = dot(mine, mine, 0, 0, precise) + dot(other, other, 0, 0, precise)
    invert_factor(gram, work_ref, inverse_ref)
    inverse = inverse_ref[...]
    for ref, part in ((mine_ref, core), (other_ref, 1 - core)):
        start = pl.multiple_of(part * HALF, HALF)
        out_ref[pl.ds(start, HALF), :] = split(dot(ref[...], inverse, 1, 1, precise))


def orthonormal(core, mine, other):
    return pl.pallas_call(
        orthonormal_kernel,
        out_shape=jax.ShapeDtypeStruct((DW, 2 * RANK), bf16),
        in_specs=[pl.BlockSpec(memory_space=pltpu.SMEM)]
        + [pl.BlockSpec(memory_space=pltpu.VMEM)] * 2,
        out_specs=pl.BlockSpec(memory_space=pltpu.VMEM),
        scratch_shapes=[pltpu.VMEM((RANK, RANK), f32), pltpu.VMEM((RANK, RANK), f32)],
        compiler_params=pltpu.CompilerParams(vmem_limit_bytes=20 * 2**20),
        cost_estimate=pl.CostEstimate(
            flops=2_000_000_000, bytes_accessed=4_000_000, transcendentals=256
        ),
        name="orthonormal",
    )(core, mine, other)


def factor_kernel(
    core_ref, error_ref, slopes_ref, mine_ref, other_ref, p_ref, *refs
):
    out_ref, turned_ref, tokens_ref, y_ref = refs[-4:]
    step = pl.program_id(0)
    core = core_ref[0]

    @pl.when(step == 0)
    def _():
        for x in range(4):
            for ref, owner in ((mine_ref, core), (other_ref, 1 - core)):
                start = pl.multiple_of((2 * x + owner) * 32, 32)
                tokens_ref[pl.ds(start, 32), :] = ref[32 * x : 32 * x + 32, :]
        y_ref[...] = split(folded(dot(tokens_ref[...], p_ref[...], 1, 0)))

    turned_ref[...] = p_ref[pl.ds(pl.multiple_of(step * 640, 640), 640), :].T
    terms = dot(error_ref[...], p_ref[...], 1, 0) + dot(slopes_ref[...], y_ref[...], 1, 0)
    rows = lax.broadcasted_iota(jnp.int32, (TILE, RANK), 0) + step * TILE
    out_ref[...] = jnp.where(rows < HIDDEN, folded(terms), 0.0).astype(bf16)


def factor_terms(core, error, slopes, mine, other, p_both, *order):
    here = pl.BlockSpec(memory_space=pltpu.VMEM)
    return pl.pallas_call(
        factor_kernel,
        grid=(4,),
        out_shape=(
            jax.ShapeDtypeStruct((4 * TILE, RANK), bf16),
            jax.ShapeDtypeStruct((2 * RANK, DW), bf16),
            jax.ShapeDtypeStruct((256, DW), bf16),
        ),
        in_specs=[
            pl.BlockSpec(memory_space=pltpu.SMEM),
            pl.BlockSpec((TILE, DW), lambda i: (i, 0)),
            pl.BlockSpec((TILE, 256), lambda i: (i, 0)),
            here,
            here,
            here,
        ]
        + [pl.BlockSpec(memory_space=pl.ANY)] * len(order),
        out_specs=(
            pl.BlockSpec((TILE, RANK), lambda i: (i, 0)),
            pl.BlockSpec((2 * RANK, 640), lambda i: (0, i)),
            here,
        ),
        scratch_shapes=[pltpu.VMEM((256, 2 * RANK), bf16)],
        compiler_params=pltpu.CompilerParams(vmem_limit_bytes=20 * 2**20),
        cost_estimate=pl.CostEstimate(
            flops=2 * 1024 * DW * 256, bytes_accessed=8_000_000, transcendentals=0
        ),
        name="factor_terms",
    )(core, error, slopes, mine, other, p_both, *order)


def residual_kernel(error_ref, slopes_ref, tokens_ref, turned_ref, q_ref, out_ref, factor_ref):
    q = q_ref[...]
    factor_ref[...] = q.astype(f32)
    left = jnp.concatenate([slopes_ref[...], -q, -q], axis=1)
    for i in range(DW // 512):
        columns = slice(512 * i, 512 * i + 512)
        right = jnp.concatenate([tokens_ref[:, columns], turned_ref[:, columns]], axis=0)
        values = error_ref[:, columns].astype(f32) + dot(left, right, 1, 0)
        out_ref[:, columns] = values.astype(bf16)


def residual(error, slopes, tokens, turned, q_factor):
    here = pl.BlockSpec(memory_space=pltpu.VMEM)
    rows = 496
    return pl.pallas_call(
        residual_kernel,
        grid=(HIDDEN // rows,),
        out_shape=(
            jax.ShapeDtypeStruct((HIDDEN, DW), bf16),
            jax.ShapeDtypeStruct((HIDDEN, RANK), f32),
        ),
        in_specs=[
            pl.BlockSpec((rows, DW), lambda i: (i, 0)),
            pl.BlockSpec((rows, 256), lambda i: (i, 0)),
            here,
            here,
            pl.BlockSpec((rows, RANK), lambda i: (i, 0)),
        ],
        out_specs=[
            pl.BlockSpec((rows, DW), lambda i: (i, 0)),
            pl.BlockSpec((rows, RANK), lambda i: (i, 0)),
        ],
        compiler_params=pltpu.CompilerParams(vmem_limit_bytes=LARGE),
        cost_estimate=pl.CostEstimate(
            flops=4 * 1024 * DW * 256, bytes_accessed=12_000_000, transcendentals=0
        ),
        name="residual",
    )(error, slopes, tokens, turned, q_factor)


def mean_kernel(blocks_ref, out_ref):
    mean = jnp.sum(blocks_ref[...].astype(f32), axis=0) / 32
    out_ref[...] = jnp.broadcast_to(mean.astype(bf16)[None], out_ref.shape)


def mean_copies(blocks):
    here = pl.BlockSpec(memory_space=pltpu.VMEM)
    return pl.pallas_call(
        mean_kernel,
        out_shape=jax.ShapeDtypeStruct(blocks.shape, bf16),
        in_specs=[here],
        out_specs=here,
        compiler_params=pltpu.CompilerParams(vmem_limit_bytes=8 * 2**20),
        cost_estimate=pl.CostEstimate(flops=200_000, bytes_accessed=600_000, transcendentals=0),
        name="mean_copies",
    )(blocks)


def grad_kernel(core_ref, slopes_ref, weights_ref, order_ref, own_ref, pair_ref, full_ref):
    del order_ref
    core = core_ref[0]
    full_ref[...] = dot(slopes_ref[...], weights_ref[...], 0, 1)
    for x in range(4):
        for ref, owner in ((own_ref, core), (pair_ref, 1 - core)):
            start = pl.multiple_of((2 * x + owner) * 32, 32)
            ref[32 * x : 32 * x + 32, :] = full_ref[pl.ds(start, 32), :]


def grad_terms(core, slopes, weights, order):
    width = 512
    return pl.pallas_call(
        grad_kernel,
        grid=(DW // width,),
        out_shape=(jax.ShapeDtypeStruct((128, DW), f32), jax.ShapeDtypeStruct((128, DW), f32)),
        in_specs=[
            pl.BlockSpec(memory_space=pltpu.SMEM),
            pl.BlockSpec(memory_space=pltpu.VMEM),
            pl.BlockSpec((width, HIDDEN), lambda i: (i, 0)),
            pl.BlockSpec(memory_space=pl.ANY),
        ],
        out_specs=[pl.BlockSpec((128, width), lambda i: (0, i))] * 2,
        scratch_shapes=[pltpu.VMEM((256, width), f32)],
        compiler_params=pltpu.CompilerParams(vmem_limit_bytes=16 * 2**20),
        cost_estimate=pl.CostEstimate(
            flops=2 * 256 * HIDDEN * DW, bytes_accessed=8_000_000, transcendentals=0
        ),
        name="grad_terms",
    )(core, slopes, weights, order)


def token_owners_sum(own):
    x = lax.axis_index("tensor") // 2

    def block(step):
        return lax.dynamic_index_in_dim(own, (x + step) % 4, 0, keepdims=False)

    total = block(0)
    for step in range(1, 4):
        pairs = [(i, (i + 2 * step) % 8) for i in range(8)]
        total = total + lax.ppermute(block(step).astype(bf16), "tensor", pairs).astype(f32)
    return total.astype(bf16)


def on_device(inputs, pre_act, grad_hidden, up_weight, error_in, q_prev):
    replicas = lax.axis_size("replica")
    core = (lax.axis_index("tensor") % 2).astype(jnp.int32)
    flag = core.reshape(1)
    error = error_in[0].T
    with jax.named_scope("gathers"):
        weights = lax.all_gather(up_weight, "replica", axis=0, tiled=True)
        slopes = hidden_slope(pre_act.T, grad_hidden.T)
        mine = broadcast_exchange(inputs, 4, "tensor", X_GROUPS).reshape(128, DW)
        other = lax.ppermute(mine, "tensor", CORE_PAIRS)
    with jax.named_scope("basis"):
        q_both = split_outside(q_prev)
        errors, own, pair = front_terms(flag, error, slopes, q_both)
        got = lax.ppermute(pair, "tensor", CORE_PAIRS)
        kept, sent = left_terms(flag, mine, own, got, errors)
        kept = kept + lax.ppermute(sent, "tensor", CORE_PAIRS)
        rows = lax.all_to_all(
            kept.reshape(16, HALF // 16, RANK), BOTH, 0, 0, axis_index_groups=XY_GROUPS
        )
        rows = jnp.sum(rows, axis=0)
        rows = jnp.sum(broadcast_exchange(rows, 8, "replica", Z_GROUPS), axis=0) / replicas
        half = broadcast_exchange(rows, 16, BOTH, XY_GROUPS).reshape(HALF, RANK)
    p_both = orthonormal(flag, half, lax.ppermute(half, "tensor", CORE_PAIRS))
    with jax.named_scope("right_factor"):
        terms, turned, tokens = factor_terms(flag, error, slopes, mine, other, p_both)
        blocks = lax.all_to_all(terms.reshape(32, 32, RANK), "replica", 0, 0)
        copies = mean_copies(blocks)
        q_block = lax.all_to_all(copies, "replica", 0, 0).reshape(1024, RANK)
    error_out, q_factor = residual(error, slopes, tokens, turned, q_block)
    with jax.named_scope("input_grad"):
        own, pair = grad_terms(flag, slopes, weights, terms)
        own = own + lax.ppermute(after(pair, copies), "tensor", CORE_PAIRS)
        input_grad = token_owners_sum(own.reshape(4, 32, DW))
    return (input_grad, q_factor, error_out.T[None])


def solution(mesh):
    placed = (
        P(("replica", "tensor"), None),
        P("replica", "tensor"),
        P("replica", "tensor"),
        P("replica", "tensor"),
        P("replica", None, "tensor"),
        P("tensor", None),
    )
    return jax.shard_map(
        on_device,
        mesh=mesh,
        in_specs=placed,
        out_specs=(P(("replica", "tensor"), None), P("tensor", None), P("replica", None, "tensor")),
        check_vma=False,
    )
```

```python
import jax
import jax.numpy as jnp
from jax import lax
from jax.experimental import pallas as pl
from jax.experimental.pallas import tpu as pltpu
from jax.sharding import PartitionSpec as P

f32, bf16 = jnp.float32, jnp.bfloat16
precise = lax.Precision.HIGHEST
root_half = 0.7071067811865476
inverse_root = 0.3989422804014327

RANK = 128
DW = 2560
HALF = DW // 2
HIDDEN = 992
TILE = 256
LARGE = 60 * 2**20
CORE_PAIRS = [(i, i ^ 1) for i in range(8)]
X_GROUPS = [[core + 2 * x for x in range(4)] for core in range(2)]
XY_GROUPS = [
    [((y * 8 + z) * 4 + x) * 2 + core for y in range(4) for x in range(4)]
    for z in range(8)
    for core in range(2)
]
Z_GROUPS = [[y * 8 + z for z in range(8)] for y in range(4)]
BOTH = ("replica", "tensor")


def hidden_slope(pre_act, grad_hidden):
    values = pre_act.astype(f32)
    normal_cdf = 0.5 * (1.0 + jax.scipy.special.erf(values * root_half))
    density = jnp.exp(-0.5 * values * values) * inverse_root
    return (grad_hidden.astype(f32) * (normal_cdf + values * density)).astype(bf16)


def dot(left, right, left_dim, right_dim, precision=None):
    return lax.dot_general(
        left,
        right,
        (((left_dim,), (right_dim,)), ((), ())),
        precision=precision,
        preferred_element_type=f32,
    )


def split_outside(values):
    high = lax.reduce_precision(values, 8, 7)
    return jnp.concatenate([high.astype(bf16), (values - high).astype(bf16)], axis=1)


def split(values):
    high = values.astype(bf16)
    return jnp.concatenate([high, (values - high.astype(f32)).astype(bf16)], axis=1)


def folded(both):
    return both[:, :RANK] + both[:, RANK:]


def broadcast_exchange(block, count, axis, groups=None):
    blocks = jnp.broadcast_to(block[None], (count, *block.shape))
    return lax.all_to_all(blocks, axis, 0, 0, axis_index_groups=groups)


def whole(shape, memory=pltpu.VMEM):
    return pl.BlockSpec(shape, lambda *_: (0,) * len(shape), memory_space=memory)


def after(values, order):
    return pl.pallas_call(
        lambda values_ref, order_ref, out_ref: None,
        out_shape=jax.ShapeDtypeStruct(values.shape, values.dtype),
        in_specs=[pl.BlockSpec(memory_space=pl.ANY)] * 2,
        out_specs=pl.BlockSpec(memory_space=pl.ANY),
        input_output_aliases={0: 0},
        cost_estimate=pl.CostEstimate(flops=1000, bytes_accessed=1000, transcendentals=0),
        name="after",
    )(values, order)


def front_kernel(core_ref, error_ref, slopes_ref, q_ref, error_out_ref, own_ref, pair_ref, z_ref):
    core = core_ref[0]

    @pl.when(pl.program_id(0) == 0)
    def _():
        z_ref[...] = folded(dot(slopes_ref[...], q_ref[...], 0, 0))
        for x in range(4):
            for ref, owner in ((own_ref, core), (pair_ref, 1 - core)):
                start = pl.multiple_of((2 * x + owner) * 32, 32)
                ref[32 * x : 32 * x + 32, :] = z_ref[pl.ds(start, 32), :]

    error_out_ref[...] = folded(dot(error_ref[...], q_ref[...], 0, 0))


def front_terms(core, error, slopes, q_both):
    here = pl.BlockSpec(memory_space=pltpu.VMEM)
    return pl.pallas_call(
        front_kernel,
        grid=(5,),
        out_shape=(
            jax.ShapeDtypeStruct((DW, RANK), f32),
            jax.ShapeDtypeStruct((128, RANK), f32),
            jax.ShapeDtypeStruct((128, RANK), f32),
        ),
        in_specs=[
            pl.BlockSpec(memory_space=pltpu.SMEM),
            pl.BlockSpec((HIDDEN, 512), lambda i: (0, i)),
            here,
            here,
        ],
        out_specs=[pl.BlockSpec((512, RANK), lambda i: (i, 0)), here, here],
        scratch_shapes=[pltpu.VMEM((256, RANK), f32)],
        compiler_params=pltpu.CompilerParams(vmem_limit_bytes=20 * 2**20),
        cost_estimate=pl.CostEstimate(
            flops=2 * HIDDEN * DW * 256, bytes_accessed=7_000_000, transcendentals=0
        ),
        name="front_terms",
    )(core, error, slopes, q_both)


def terms_kernel(core_ref, mine_ref, own_ref, got_ref, error_ref, kept_ref, sent_ref):
    core = core_ref[0]
    both = split(own_ref[...] + got_ref[...])
    for ref, part in ((kept_ref, core), (sent_ref, 1 - core)):
        start = pl.multiple_of(part * HALF, HALF)
        columns = mine_ref[:, pl.ds(start, HALF)]
        ref[...] = folded(dot(columns, both, 0, 0)) + error_ref[pl.ds(start, HALF), :]


def left_terms(core, mine, own, got, errors):
    return pl.pallas_call(
        terms_kernel,
        out_shape=(
            jax.ShapeDtypeStruct((HALF, RANK), f32),
            jax.ShapeDtypeStruct((HALF, RANK), f32),
        ),
        in_specs=[pl.BlockSpec(memory_space=pltpu.SMEM)]
        + [pl.BlockSpec(memory_space=pltpu.VMEM)] * 4,
        out_specs=[pl.BlockSpec(memory_space=pltpu.VMEM)] * 2,
        compiler_params=pltpu.CompilerParams(vmem_limit_bytes=20 * 2**20),
        cost_estimate=pl.CostEstimate(
            flops=2 * 128 * DW * 256, bytes_accessed=4_000_000, transcendentals=0
        ),
        name="left_terms",
    )(core, mine, own, got, errors)


def invert_factor(gram, work_ref, out_ref):
    sub = lax.broadcasted_iota(jnp.int32, (8, RANK), 0)
    lane = lax.broadcasted_iota(jnp.int32, (8, RANK), 1)
    work_ref[...] = gram

    def spread(rows, column):
        return jnp.broadcast_to(rows[:, column : column + 1], (8, RANK))

    def row(values, k):
        return jnp.broadcast_to(values[k : k + 1, :], (8, RANK))

    current = work_ref[0:8, :]
    for r in range(16):
        base = 8 * r
        last = r == 15
        inside = (lane >= base) & (lane < base + 8)
        columns = [spread(current, base + k) for k in range(8)]
        current = jnp.where(inside, jnp.where(lane - base == sub, 1.0, 0.0), current)
        if not last:
            after = work_ref[base + 8 : base + 16, :]
            after_columns = [spread(after, base + k) for k in range(8)]
            after = jnp.where(inside, 0.0, after)
        inverse = jnp.zeros((8, RANK), f32)
        for k in range(8):
            pivot_inverse = 1.0 / row(columns[k], k)
            ratio = jnp.where(sub > k, columns[k] * pivot_inverse, 0.0)
            inverse = jnp.where(sub == k, pivot_inverse, inverse)
            pivot_row = row(current, k)
            current = current - ratio * pivot_row
            tops = {i: row(columns[i], k) for i in range(k + 1, 8)}
            for i in range(k + 1, 8):
                columns[i] = columns[i] - ratio * tops[i]
            if not last:
                ratio = after_columns[k] * pivot_inverse
                for i in range(k + 1, 8):
                    after_columns[i] = after_columns[i] - ratio * tops[i]
                after = after - ratio * pivot_row
        out_ref[base : base + 8, :] = jnp.where(lane < base + 8, current * lax.sqrt(inverse), 0.0)
        if r < 14:
            top = base + 16
            scaled = jnp.where(lane >= top, current * inverse, 0.0)
            update = dot(scaled, current, 0, 0, precise)
            lanes = lax.broadcasted_iota(jnp.int32, (RANK - top, RANK), 1)
            rest = jnp.where((lanes >= base) & (lanes < base + 8), 0.0, work_ref[top:, :])
            work_ref[top:, :] = rest - update[top:, :]
        if not last:
            current = after


def orthonormal_kernel(core_ref, mine_ref, other_ref, out_ref, work_ref, inverse_ref):
    core = core_ref[0]
    mine, other = mine_ref[...], other_ref[...]
    gram = dot(mine, mine, 0, 0, precise) + dot(other, other, 0, 0, precise)
    invert_factor(gram, work_ref, inverse_ref)
    inverse = inverse_ref[...]
    for ref, part in ((mine_ref, core), (other_ref, 1 - core)):
        start = pl.multiple_of(part * HALF, HALF)
        out_ref[pl.ds(start, HALF), :] = split(dot(ref[...], inverse, 1, 1, precise))


def orthonormal(core, mine, other):
    return pl.pallas_call(
        orthonormal_kernel,
        out_shape=jax.ShapeDtypeStruct((DW, 2 * RANK), bf16),
        in_specs=[pl.BlockSpec(memory_space=pltpu.SMEM)]
        + [pl.BlockSpec(memory_space=pltpu.VMEM)] * 2,
        out_specs=pl.BlockSpec(memory_space=pltpu.VMEM),
        scratch_shapes=[pltpu.VMEM((RANK, RANK), f32), pltpu.VMEM((RANK, RANK), f32)],
        compiler_params=pltpu.CompilerParams(vmem_limit_bytes=20 * 2**20),
        cost_estimate=pl.CostEstimate(
            flops=2_000_000_000, bytes_accessed=4_000_000, transcendentals=256
        ),
        name="orthonormal",
    )(core, mine, other)


def factor_kernel(
    core_ref, error_ref, slopes_ref, mine_ref, other_ref, p_ref, *refs
):
    out_ref, tokens_ref, y_ref = refs[-3:]
    step = pl.program_id(0)
    core = core_ref[0]

    @pl.when(step == 0)
    def _():
        for x in range(4):
            for ref, owner in ((mine_ref, core), (other_ref, 1 - core)):
                start = pl.multiple_of((2 * x + owner) * 32, 32)
                tokens_ref[pl.ds(start, 32), :] = ref[32 * x : 32 * x + 32, :]
        y_ref[...] = split(folded(dot(tokens_ref[...], p_ref[...], 1, 0)))

    terms = dot(error_ref[...], p_ref[...], 1, 0) + dot(slopes_ref[...], y_ref[...], 1, 0)
    rows = lax.broadcasted_iota(jnp.int32, (TILE, RANK), 0) + step * TILE
    out_ref[...] = jnp.where(rows < HIDDEN, folded(terms), 0.0).astype(bf16)


def factor_terms(core, error, slopes, mine, other, p_both, *order):
    here = pl.BlockSpec(memory_space=pltpu.VMEM)
    return pl.pallas_call(
        factor_kernel,
        grid=(4,),
        out_shape=(
            jax.ShapeDtypeStruct((4 * TILE, RANK), bf16),
        ),
        in_specs=[
            pl.BlockSpec(memory_space=pltpu.SMEM),
            pl.BlockSpec((TILE, DW), lambda i: (i, 0)),
            pl.BlockSpec((TILE, 256), lambda i: (i, 0)),
            here,
            here,
            here,
        ]
        + [pl.BlockSpec(memory_space=pl.ANY)] * len(order),
        out_specs=(
            pl.BlockSpec((TILE, RANK), lambda i: (i, 0)),
        ),
        scratch_shapes=[pltpu.VMEM((256, DW), bf16), pltpu.VMEM((256, 2 * RANK), bf16)],
        compiler_params=pltpu.CompilerParams(vmem_limit_bytes=20 * 2**20),
        cost_estimate=pl.CostEstimate(
            flops=2 * 1024 * DW * 256, bytes_accessed=8_000_000, transcendentals=0
        ),
        name="factor_terms",
    )(core, error, slopes, mine, other, p_both, *order)


def turn_kernel(p_ref, order_ref, out_ref):
    del order_ref
    out_ref[...] = p_ref[...].T


def turned_after(p_both, order):
    here = pl.BlockSpec(memory_space=pltpu.VMEM)
    return pl.pallas_call(
        turn_kernel,
        out_shape=jax.ShapeDtypeStruct((2 * RANK, DW), bf16),
        in_specs=[here, pl.BlockSpec(memory_space=pl.ANY)],
        out_specs=here,
        compiler_params=pltpu.CompilerParams(vmem_limit_bytes=8 * 2**20),
        cost_estimate=pl.CostEstimate(
            flops=1_000_000, bytes_accessed=20_000_000, transcendentals=0
        ),
        name="turned_after",
    )(p_both, order)


def residual_kernel(
    core_ref, error_ref, slopes_ref, mine_ref, other_ref, turned_ref, q_ref, out_ref, factor_ref, tokens_ref
):
    core = core_ref[0]

    @pl.when(pl.program_id(0) == 0)
    def _():
        for x in range(4):
            for ref, owner in ((mine_ref, core), (other_ref, 1 - core)):
                start = pl.multiple_of((2 * x + owner) * 32, 32)
                tokens_ref[pl.ds(start, 32), :] = ref[32 * x : 32 * x + 32, :]

    q = q_ref[...]
    factor_ref[...] = q.astype(f32)
    left = jnp.concatenate([slopes_ref[...], -q, -q], axis=1)
    for i in range(DW // 512):
        columns = slice(512 * i, 512 * i + 512)
        right = jnp.concatenate([tokens_ref[:, columns], turned_ref[:, columns]], axis=0)
        values = error_ref[:, columns].astype(f32) + dot(left, right, 1, 0)
        out_ref[:, columns] = values.astype(bf16)


def residual(core, error, slopes, mine, other, turned, q_factor):
    here = pl.BlockSpec(memory_space=pltpu.VMEM)
    rows = 496
    return pl.pallas_call(
        residual_kernel,
        grid=(HIDDEN // rows,),
        out_shape=(
            jax.ShapeDtypeStruct((HIDDEN, DW), bf16),
            jax.ShapeDtypeStruct((HIDDEN, RANK), f32),
        ),
        in_specs=[
            pl.BlockSpec(memory_space=pltpu.SMEM),
            pl.BlockSpec((rows, DW), lambda i: (i, 0)),
            pl.BlockSpec((rows, 256), lambda i: (i, 0)),
            here,
            here,
            here,
            pl.BlockSpec((rows, RANK), lambda i: (i, 0)),
        ],
        out_specs=[
            pl.BlockSpec((rows, DW), lambda i: (i, 0)),
            pl.BlockSpec((rows, RANK), lambda i: (i, 0)),
        ],
        scratch_shapes=[pltpu.VMEM((256, DW), bf16)],
        compiler_params=pltpu.CompilerParams(vmem_limit_bytes=LARGE),
        cost_estimate=pl.CostEstimate(
            flops=4 * 1024 * DW * 256, bytes_accessed=12_000_000, transcendentals=0
        ),
        name="residual",
    )(core, error, slopes, mine, other, turned, q_factor)


def mean_kernel(blocks_ref, out_ref):
    mean = jnp.sum(blocks_ref[...].astype(f32), axis=0) / 32
    out_ref[...] = jnp.broadcast_to(mean.astype(bf16)[None], out_ref.shape)


def mean_copies(blocks):
    here = pl.BlockSpec(memory_space=pltpu.VMEM)
    return pl.pallas_call(
        mean_kernel,
        out_shape=jax.ShapeDtypeStruct(blocks.shape, bf16),
        in_specs=[here],
        out_specs=here,
        compiler_params=pltpu.CompilerParams(vmem_limit_bytes=8 * 2**20),
        cost_estimate=pl.CostEstimate(flops=200_000, bytes_accessed=600_000, transcendentals=0),
        name="mean_copies",
    )(blocks)


def grad_kernel(core_ref, slopes_ref, weights_ref, order_ref, own_ref, pair_ref, full_ref):
    del order_ref
    core = core_ref[0]
    full_ref[...] = dot(slopes_ref[...], weights_ref[...], 0, 1)
    for x in range(4):
        for ref, owner in ((own_ref, core), (pair_ref, 1 - core)):
            start = pl.multiple_of((2 * x + owner) * 32, 32)
            ref[32 * x : 32 * x + 32, :] = full_ref[pl.ds(start, 32), :]


def grad_terms(core, slopes, weights, order):
    width = 512
    return pl.pallas_call(
        grad_kernel,
        grid=(DW // width,),
        out_shape=(jax.ShapeDtypeStruct((128, DW), f32), jax.ShapeDtypeStruct((128, DW), f32)),
        in_specs=[
            pl.BlockSpec(memory_space=pltpu.SMEM),
            pl.BlockSpec(memory_space=pltpu.VMEM),
            pl.BlockSpec((width, HIDDEN), lambda i: (i, 0)),
            pl.BlockSpec(memory_space=pl.ANY),
        ],
        out_specs=[pl.BlockSpec((128, width), lambda i: (0, i))] * 2,
        scratch_shapes=[pltpu.VMEM((256, width), f32)],
        compiler_params=pltpu.CompilerParams(vmem_limit_bytes=LARGE - 9 * 2**18),
        cost_estimate=pl.CostEstimate(
            flops=2 * 256 * HIDDEN * DW, bytes_accessed=8_000_000, transcendentals=0
        ),
        name="grad_terms",
    )(core, slopes, weights, order)


def token_owners_sum(own):
    x = lax.axis_index("tensor") // 2

    def block(step):
        return lax.dynamic_index_in_dim(own, (x + step) % 4, 0, keepdims=False)

    total = block(0)
    for step in range(1, 4):
        pairs = [(i, (i + 2 * step) % 8) for i in range(8)]
        total = total + lax.ppermute(block(step).astype(bf16), "tensor", pairs).astype(f32)
    return total.astype(bf16)


def on_device(inputs, pre_act, grad_hidden, up_weight, error_in, q_prev):
    replicas = lax.axis_size("replica")
    core = (lax.axis_index("tensor") % 2).astype(jnp.int32)
    flag = core.reshape(1)
    error = error_in[0].T
    with jax.named_scope("gathers"):
        weights = lax.all_gather(up_weight, "replica", axis=0, tiled=True)
        slopes = hidden_slope(pre_act.T, grad_hidden.T)
        mine = broadcast_exchange(inputs, 4, "tensor", X_GROUPS).reshape(128, DW)
        other = lax.ppermute(mine, "tensor", CORE_PAIRS)
    with jax.named_scope("basis"):
        q_both = split_outside(q_prev)
        errors, own, pair = front_terms(flag, error, slopes, q_both)
        got = lax.ppermute(pair, "tensor", CORE_PAIRS)
        kept, sent = left_terms(flag, mine, own, got, errors)
        kept = kept + lax.ppermute(sent, "tensor", CORE_PAIRS)
        rows = lax.all_to_all(
            kept.reshape(16, HALF // 16, RANK), BOTH, 0, 0, axis_index_groups=XY_GROUPS
        )
        rows = jnp.sum(rows, axis=0)
        rows = jnp.sum(broadcast_exchange(rows, 8, "replica", Z_GROUPS), axis=0) / replicas
        half = broadcast_exchange(rows, 16, BOTH, XY_GROUPS).reshape(HALF, RANK)
    p_both = orthonormal(flag, half, lax.ppermute(half, "tensor", CORE_PAIRS))
    with jax.named_scope("right_factor"):
        (terms,) = factor_terms(flag, error, slopes, mine, other, p_both)
        blocks = lax.all_to_all(terms.reshape(32, 32, RANK), "replica", 0, 0)
        copies = mean_copies(blocks)
        turned = turned_after(p_both, copies)
        q_block = lax.all_to_all(copies, "replica", 0, 0).reshape(1024, RANK)
    error_out, q_factor = residual(flag, error, slopes, mine, other, turned, q_block)
    with jax.named_scope("input_grad"):
        own, pair = grad_terms(flag, slopes, weights, terms)
        own = own + lax.ppermute(after(pair, copies), "tensor", CORE_PAIRS)
        input_grad = token_owners_sum(own.reshape(4, 32, DW))
    return (input_grad, q_factor, error_out.T[None])


def solution(mesh):
    placed = (
        P(("replica", "tensor"), None),
        P("replica", "tensor"),
        P("replica", "tensor"),
        P("replica", "tensor"),
        P("replica", None, "tensor"),
        P("tensor", None),
    )
    return jax.shard_map(
        on_device,
        mesh=mesh,
        in_specs=placed,
        out_specs=(P(("replica", "tensor"), None), P("tensor", None), P("replica", None, "tensor")),
        check_vma=False,
    )
```

```python
import jax
import jax.numpy as jnp
from jax import lax
from jax.experimental import pallas as pl
from jax.experimental.pallas import tpu as pltpu
from jax.sharding import PartitionSpec as P

f32, bf16 = jnp.float32, jnp.bfloat16
precise = lax.Precision.HIGHEST
root_half = 0.7071067811865476
inverse_root = 0.3989422804014327

RANK = 128
DW = 2560
HALF = DW // 2
HIDDEN = 992
TILE = 256
LARGE = 60 * 2**20
CORE_PAIRS = [(i, i ^ 1) for i in range(8)]
X_GROUPS = [[core + 2 * x for x in range(4)] for core in range(2)]
XY_GROUPS = [
    [((y * 8 + z) * 4 + x) * 2 + core for y in range(4) for x in range(4)]
    for z in range(8)
    for core in range(2)
]
Z_GROUPS = [[y * 8 + z for z in range(8)] for y in range(4)]
BOTH = ("replica", "tensor")


def hidden_slope(pre_act, grad_hidden):
    values = pre_act.astype(f32)
    normal_cdf = 0.5 * (1.0 + jax.scipy.special.erf(values * root_half))
    density = jnp.exp(-0.5 * values * values) * inverse_root
    return (grad_hidden.astype(f32) * (normal_cdf + values * density)).astype(bf16)


def dot(left, right, left_dim, right_dim, precision=None):
    return lax.dot_general(
        left,
        right,
        (((left_dim,), (right_dim,)), ((), ())),
        precision=precision,
        preferred_element_type=f32,
    )


def split_outside(values):
    high = lax.reduce_precision(values, 8, 7)
    return jnp.concatenate([high.astype(bf16), (values - high).astype(bf16)], axis=1)


def split(values):
    high = values.astype(bf16)
    return jnp.concatenate([high, (values - high.astype(f32)).astype(bf16)], axis=1)


def folded(both):
    return both[:, :RANK] + both[:, RANK:]


def broadcast_exchange(block, count, axis, groups=None):
    blocks = jnp.broadcast_to(block[None], (count, *block.shape))
    return lax.all_to_all(blocks, axis, 0, 0, axis_index_groups=groups)


def whole(shape, memory=pltpu.VMEM):
    return pl.BlockSpec(shape, lambda *_: (0,) * len(shape), memory_space=memory)


def after(values, order):
    return pl.pallas_call(
        lambda values_ref, order_ref, out_ref: None,
        out_shape=jax.ShapeDtypeStruct(values.shape, values.dtype),
        in_specs=[pl.BlockSpec(memory_space=pl.ANY)] * 2,
        out_specs=pl.BlockSpec(memory_space=pl.ANY),
        input_output_aliases={0: 0},
        cost_estimate=pl.CostEstimate(flops=1000, bytes_accessed=1000, transcendentals=0),
        name="after",
    )(values, order)


def front_kernel(
    core_ref, error_ref, slopes_ref, q_ref, error_out_ref, own_ref, pair_ref, z_ref, both_ref
):
    core = core_ref[0]

    @pl.when(pl.program_id(0) == 0)
    def _():
        both_ref[...] = split(q_ref[...])
        z_ref[...] = folded(dot(slopes_ref[...], both_ref[...], 0, 0))
        for x in range(4):
            for ref, owner in ((own_ref, core), (pair_ref, 1 - core)):
                start = pl.multiple_of((2 * x + owner) * 32, 32)
                ref[32 * x : 32 * x + 32, :] = z_ref[pl.ds(start, 32), :]

    error_out_ref[...] = folded(dot(error_ref[...], both_ref[...], 0, 0))


def front_terms(core, error, slopes, q_both):
    here = pl.BlockSpec(memory_space=pltpu.VMEM)
    return pl.pallas_call(
        front_kernel,
        grid=(5,),
        out_shape=(
            jax.ShapeDtypeStruct((DW, RANK), f32),
            jax.ShapeDtypeStruct((128, RANK), f32),
            jax.ShapeDtypeStruct((128, RANK), f32),
        ),
        in_specs=[
            pl.BlockSpec(memory_space=pltpu.SMEM),
            pl.BlockSpec((HIDDEN, 512), lambda i: (0, i)),
            here,
            here,
        ],
        out_specs=[pl.BlockSpec((512, RANK), lambda i: (i, 0)), here, here],
        scratch_shapes=[pltpu.VMEM((256, RANK), f32), pltpu.VMEM((HIDDEN, 2 * RANK), bf16)],
        compiler_params=pltpu.CompilerParams(vmem_limit_bytes=20 * 2**20),
        cost_estimate=pl.CostEstimate(
            flops=2 * HIDDEN * DW * 256, bytes_accessed=7_000_000, transcendentals=0
        ),
        name="front_terms",
    )(core, error, slopes, q_both)


def terms_kernel(core_ref, mine_ref, own_ref, got_ref, error_ref, kept_ref, sent_ref):
    core = core_ref[0]
    both = split(own_ref[...] + got_ref[...])
    for ref, part in ((kept_ref, core), (sent_ref, 1 - core)):
        start = pl.multiple_of(part * HALF, HALF)
        columns = mine_ref[:, pl.ds(start, HALF)]
        ref[...] = folded(dot(columns, both, 0, 0)) + error_ref[pl.ds(start, HALF), :]


def left_terms(core, mine, own, got, errors):
    return pl.pallas_call(
        terms_kernel,
        out_shape=(
            jax.ShapeDtypeStruct((HALF, RANK), f32),
            jax.ShapeDtypeStruct((HALF, RANK), f32),
        ),
        in_specs=[pl.BlockSpec(memory_space=pltpu.SMEM)]
        + [pl.BlockSpec(memory_space=pltpu.VMEM)] * 4,
        out_specs=[pl.BlockSpec(memory_space=pltpu.VMEM)] * 2,
        compiler_params=pltpu.CompilerParams(vmem_limit_bytes=20 * 2**20),
        cost_estimate=pl.CostEstimate(
            flops=2 * 128 * DW * 256, bytes_accessed=4_000_000, transcendentals=0
        ),
        name="left_terms",
    )(core, mine, own, got, errors)


def invert_factor(gram, work_ref, out_ref):
    sub = lax.broadcasted_iota(jnp.int32, (8, RANK), 0)
    lane = lax.broadcasted_iota(jnp.int32, (8, RANK), 1)
    work_ref[...] = gram

    def spread(rows, column):
        return jnp.broadcast_to(rows[:, column : column + 1], (8, RANK))

    def row(values, k):
        return jnp.broadcast_to(values[k : k + 1, :], (8, RANK))

    current = work_ref[0:8, :]
    for r in range(16):
        base = 8 * r
        last = r == 15
        inside = (lane >= base) & (lane < base + 8)
        columns = [spread(current, base + k) for k in range(8)]
        current = jnp.where(inside, jnp.where(lane - base == sub, 1.0, 0.0), current)
        if not last:
            after = work_ref[base + 8 : base + 16, :]
            after_columns = [spread(after, base + k) for k in range(8)]
            after = jnp.where(inside, 0.0, after)
        inverse = jnp.zeros((8, RANK), f32)
        for k in range(8):
            pivot_inverse = 1.0 / row(columns[k], k)
            ratio = jnp.where(sub > k, columns[k] * pivot_inverse, 0.0)
            inverse = jnp.where(sub == k, pivot_inverse, inverse)
            pivot_row = row(current, k)
            current = current - ratio * pivot_row
            tops = {i: row(columns[i], k) for i in range(k + 1, 8)}
            for i in range(k + 1, 8):
                columns[i] = columns[i] - ratio * tops[i]
            if not last:
                ratio = after_columns[k] * pivot_inverse
                for i in range(k + 1, 8):
                    after_columns[i] = after_columns[i] - ratio * tops[i]
                after = after - ratio * pivot_row
        out_ref[base : base + 8, :] = jnp.where(lane < base + 8, current * lax.sqrt(inverse), 0.0)
        if r < 14:
            top = base + 16
            scaled = jnp.where(lane >= top, current * inverse, 0.0)
            update = dot(scaled, current, 0, 0, precise)
            lanes = lax.broadcasted_iota(jnp.int32, (RANK - top, RANK), 1)
            rest = jnp.where((lanes >= base) & (lanes < base + 8), 0.0, work_ref[top:, :])
            work_ref[top:, :] = rest - update[top:, :]
        if not last:
            current = after


def orthonormal_kernel(core_ref, mine_ref, other_ref, out_ref, work_ref, inverse_ref):
    core = core_ref[0]
    mine, other = mine_ref[...], other_ref[...]
    gram = dot(mine, mine, 0, 0, precise) + dot(other, other, 0, 0, precise)
    invert_factor(gram, work_ref, inverse_ref)
    inverse = inverse_ref[...]
    for ref, part in ((mine_ref, core), (other_ref, 1 - core)):
        start = pl.multiple_of(part * HALF, HALF)
        out_ref[pl.ds(start, HALF), :] = split(dot(ref[...], inverse, 1, 1, precise))


def orthonormal(core, mine, other):
    return pl.pallas_call(
        orthonormal_kernel,
        out_shape=jax.ShapeDtypeStruct((DW, 2 * RANK), bf16),
        in_specs=[pl.BlockSpec(memory_space=pltpu.SMEM)]
        + [pl.BlockSpec(memory_space=pltpu.VMEM)] * 2,
        out_specs=pl.BlockSpec(memory_space=pltpu.VMEM),
        scratch_shapes=[pltpu.VMEM((RANK, RANK), f32), pltpu.VMEM((RANK, RANK), f32)],
        compiler_params=pltpu.CompilerParams(vmem_limit_bytes=20 * 2**20),
        cost_estimate=pl.CostEstimate(
            flops=2_000_000_000, bytes_accessed=4_000_000, transcendentals=256
        ),
        name="orthonormal",
    )(core, mine, other)


def factor_kernel(
    core_ref, error_ref, slopes_ref, mine_ref, other_ref, p_ref, *refs
):
    out_ref, tokens_ref, y_ref = refs[-3:]
    step = pl.program_id(0)
    core = core_ref[0]

    @pl.when(step == 0)
    def _():
        for x in range(4):
            for ref, owner in ((mine_ref, core), (other_ref, 1 - core)):
                start = pl.multiple_of((2 * x + owner) * 32, 32)
                tokens_ref[pl.ds(start, 32), :] = ref[32 * x : 32 * x + 32, :]
        y_ref[...] = split(folded(dot(tokens_ref[...], p_ref[...], 1, 0)))

    terms = dot(error_ref[...], p_ref[...], 1, 0) + dot(slopes_ref[...], y_ref[...], 1, 0)
    rows = lax.broadcasted_iota(jnp.int32, (TILE, RANK), 0) + step * TILE
    out_ref[...] = jnp.where(rows < HIDDEN, folded(terms), 0.0).astype(bf16)


def factor_terms(core, error, slopes, mine, other, p_both, *order):
    here = pl.BlockSpec(memory_space=pltpu.VMEM)
    return pl.pallas_call(
        factor_kernel,
        grid=(4,),
        out_shape=(
            jax.ShapeDtypeStruct((4 * TILE, RANK), bf16),
        ),
        in_specs=[
            pl.BlockSpec(memory_space=pltpu.SMEM),
            pl.BlockSpec((TILE, DW), lambda i: (i, 0)),
            pl.BlockSpec((TILE, 256), lambda i: (i, 0)),
            here,
            here,
            here,
        ]
        + [pl.BlockSpec(memory_space=pl.ANY)] * len(order),
        out_specs=(
            pl.BlockSpec((TILE, RANK), lambda i: (i, 0)),
        ),
        scratch_shapes=[pltpu.VMEM((256, DW), bf16), pltpu.VMEM((256, 2 * RANK), bf16)],
        compiler_params=pltpu.CompilerParams(vmem_limit_bytes=20 * 2**20),
        cost_estimate=pl.CostEstimate(
            flops=2 * 1024 * DW * 256, bytes_accessed=8_000_000, transcendentals=0
        ),
        name="factor_terms",
    )(core, error, slopes, mine, other, p_both, *order)


def turn_kernel(p_ref, order_ref, out_ref):
    del order_ref
    out_ref[...] = p_ref[...].T


def turned_after(p_both, order):
    here = pl.BlockSpec(memory_space=pltpu.VMEM)
    return pl.pallas_call(
        turn_kernel,
        out_shape=jax.ShapeDtypeStruct((2 * RANK, DW), bf16),
        in_specs=[here, pl.BlockSpec(memory_space=pl.ANY)],
        out_specs=here,
        compiler_params=pltpu.CompilerParams(vmem_limit_bytes=8 * 2**20),
        cost_estimate=pl.CostEstimate(
            flops=1_000_000, bytes_accessed=20_000_000, transcendentals=0
        ),
        name="turned_after",
    )(p_both, order)


def residual_kernel(
    core_ref, error_ref, slopes_ref, mine_ref, other_ref, turned_ref, q_ref, out_ref, factor_ref, tokens_ref
):
    core = core_ref[0]

    @pl.when(pl.program_id(0) == 0)
    def _():
        for x in range(4):
            for ref, owner in ((mine_ref, core), (other_ref, 1 - core)):
                start = pl.multiple_of((2 * x + owner) * 32, 32)
                tokens_ref[pl.ds(start, 32), :] = ref[32 * x : 32 * x + 32, :]

    q = q_ref[...]
    factor_ref[...] = q.astype(f32)
    left = jnp.concatenate([slopes_ref[...], -q, -q], axis=1)
    for i in range(DW // 512):
        columns = slice(512 * i, 512 * i + 512)
        right = jnp.concatenate([tokens_ref[:, columns], turned_ref[:, columns]], axis=0)
        values = error_ref[:, columns].astype(f32) + dot(left, right, 1, 0)
        out_ref[:, columns] = values.astype(bf16)


def residual(core, error, slopes, mine, other, turned, q_factor):
    here = pl.BlockSpec(memory_space=pltpu.VMEM)
    rows = 496
    return pl.pallas_call(
        residual_kernel,
        grid=(HIDDEN // rows,),
        out_shape=(
            jax.ShapeDtypeStruct((HIDDEN, DW), bf16),
            jax.ShapeDtypeStruct((HIDDEN, RANK), f32),
        ),
        in_specs=[
            pl.BlockSpec(memory_space=pltpu.SMEM),
            pl.BlockSpec((rows, DW), lambda i: (i, 0)),
            pl.BlockSpec((rows, 256), lambda i: (i, 0)),
            here,
            here,
            here,
            pl.BlockSpec((rows, RANK), lambda i: (i, 0)),
        ],
        out_specs=[
            pl.BlockSpec((rows, DW), lambda i: (i, 0)),
            pl.BlockSpec((rows, RANK), lambda i: (i, 0)),
        ],
        scratch_shapes=[pltpu.VMEM((256, DW), bf16)],
        compiler_params=pltpu.CompilerParams(vmem_limit_bytes=LARGE),
        cost_estimate=pl.CostEstimate(
            flops=4 * 1024 * DW * 256, bytes_accessed=12_000_000, transcendentals=0
        ),
        name="residual",
    )(core, error, slopes, mine, other, turned, q_factor)


def mean_kernel(blocks_ref, out_ref):
    mean = jnp.sum(blocks_ref[...].astype(f32), axis=0) / 32
    out_ref[...] = jnp.broadcast_to(mean.astype(bf16)[None], out_ref.shape)


def mean_copies(blocks):
    here = pl.BlockSpec(memory_space=pltpu.VMEM)
    return pl.pallas_call(
        mean_kernel,
        out_shape=jax.ShapeDtypeStruct(blocks.shape, bf16),
        in_specs=[here],
        out_specs=here,
        compiler_params=pltpu.CompilerParams(vmem_limit_bytes=8 * 2**20),
        cost_estimate=pl.CostEstimate(flops=200_000, bytes_accessed=600_000, transcendentals=0),
        name="mean_copies",
    )(blocks)


def grad_kernel(core_ref, slopes_ref, weights_ref, order_ref, own_ref, pair_ref, full_ref):
    del order_ref
    core = core_ref[0]
    full_ref[...] = dot(slopes_ref[...], weights_ref[...], 0, 1)
    for x in range(4):
        for ref, owner in ((own_ref, core), (pair_ref, 1 - core)):
            start = pl.multiple_of((2 * x + owner) * 32, 32)
            ref[32 * x : 32 * x + 32, :] = full_ref[pl.ds(start, 32), :]


def grad_terms(core, slopes, weights, order):
    width = 512
    return pl.pallas_call(
        grad_kernel,
        grid=(DW // width,),
        out_shape=(jax.ShapeDtypeStruct((128, DW), f32), jax.ShapeDtypeStruct((128, DW), f32)),
        in_specs=[
            pl.BlockSpec(memory_space=pltpu.SMEM),
            pl.BlockSpec(memory_space=pltpu.VMEM),
            pl.BlockSpec((width, HIDDEN), lambda i: (i, 0)),
            pl.BlockSpec(memory_space=pl.ANY),
        ],
        out_specs=[pl.BlockSpec((128, width), lambda i: (0, i))] * 2,
        scratch_shapes=[pltpu.VMEM((256, width), f32)],
        compiler_params=pltpu.CompilerParams(vmem_limit_bytes=LARGE - 9 * 2**18),
        cost_estimate=pl.CostEstimate(
            flops=2 * 256 * HIDDEN * DW, bytes_accessed=8_000_000, transcendentals=0
        ),
        name="grad_terms",
    )(core, slopes, weights, order)


def token_owners_sum(own):
    x = lax.axis_index("tensor") // 2

    def block(step):
        return lax.dynamic_index_in_dim(own, (x + step) % 4, 0, keepdims=False)

    total = block(0)
    for step in range(1, 4):
        pairs = [(i, (i + 2 * step) % 8) for i in range(8)]
        total = total + lax.ppermute(block(step).astype(bf16), "tensor", pairs).astype(f32)
    return total.astype(bf16)


def on_device(inputs, pre_act, grad_hidden, up_weight, error_in, q_prev):
    replicas = lax.axis_size("replica")
    core = (lax.axis_index("tensor") % 2).astype(jnp.int32)
    flag = core.reshape(1)
    error = error_in[0].T
    with jax.named_scope("gathers"):
        weights = lax.all_gather(up_weight, "replica", axis=0, tiled=True)
        slopes = hidden_slope(pre_act.T, grad_hidden.T)
        mine = broadcast_exchange(inputs, 4, "tensor", X_GROUPS).reshape(128, DW)
        other = lax.ppermute(mine, "tensor", CORE_PAIRS)
    with jax.named_scope("basis"):
        errors, own, pair = front_terms(flag, error, slopes, q_prev)
        got = lax.ppermute(pair, "tensor", CORE_PAIRS)
        kept, sent = left_terms(flag, mine, own, got, errors)
        kept = kept + lax.ppermute(sent, "tensor", CORE_PAIRS)
        rows = lax.all_to_all(
            kept.reshape(16, HALF // 16, RANK), BOTH, 0, 0, axis_index_groups=XY_GROUPS
        )
        rows = jnp.sum(rows, axis=0)
        rows = jnp.sum(broadcast_exchange(rows, 8, "replica", Z_GROUPS), axis=0) / replicas
        half = broadcast_exchange(rows, 16, BOTH, XY_GROUPS).reshape(HALF, RANK)
    p_both = orthonormal(flag, half, lax.ppermute(half, "tensor", CORE_PAIRS))
    with jax.named_scope("right_factor"):
        (terms,) = factor_terms(flag, error, slopes, mine, other, p_both)
        blocks = lax.all_to_all(terms.reshape(32, 32, RANK), "replica", 0, 0)
        copies = mean_copies(blocks)
        turned = turned_after(p_both, copies)
        q_block = lax.all_to_all(copies, "replica", 0, 0).reshape(1024, RANK)
    error_out, q_factor = residual(flag, error, slopes, mine, other, turned, q_block)
    with jax.named_scope("input_grad"):
        own, pair = grad_terms(flag, slopes, weights, terms)
        own = own + lax.ppermute(after(pair, copies), "tensor", CORE_PAIRS)
        input_grad = token_owners_sum(own.reshape(4, 32, DW))
    return (input_grad, q_factor, error_out.T[None])


def solution(mesh):
    placed = (
        P(("replica", "tensor"), None),
        P("replica", "tensor"),
        P("replica", "tensor"),
        P("replica", "tensor"),
        P("replica", None, "tensor"),
        P("tensor", None),
    )
    return jax.shard_map(
        on_device,
        mesh=mesh,
        in_specs=placed,
        out_specs=(P(("replica", "tensor"), None), P("tensor", None), P("replica", None, "tensor")),
        check_vma=False,
    )
```
